32 devices in a mesh: dp: 4 (over x, core), expert: 8 (over z, y).
Axes of the slice: x: 2, y: 2, z: 4, core: 2. Of those that a mesh axis runs over, the one named last changes fastest.
Arguments:
- tokens: bfloat16 [2048, 7168], P('expert', 'dp'), may hold values from -6 to 6
- grad_out: bfloat16 [2048, 7168], P('expert', 'dp'), may hold values from -6 to 6
- route_ids: int32 [2048, 8], P('expert'), may hold values from 0 to 255, all different within a row; in each aligned block of 256 rows (0 to 255, 256 to 511, ...) at most 12 rows name the same one
- route_gates: float32 [2048, 8], P('expert'), may hold values from 0.1 to 1
- w_gate: bfloat16 [8, 7168, 1024], P('expert', 'dp'), may hold values from -0.0625 to 0.0625
- w_up: bfloat16 [8, 7168, 1024], P('expert', 'dp'), may hold values from -0.0625 to 0.0625
- w_down: bfloat16 [8, 1024, 7168], P('expert', None, 'dp'), may hold values from -0.1875 to 0.1875
- shared_gate: bfloat16 [7168, 1024], P('dp', 'expert'), may hold values from -0.0625 to 0.0625
- shared_up: bfloat16 [7168, 1024], P('dp', 'expert'), may hold values from -0.0625 to 0.0625
- shared_down: bfloat16 [1024, 7168], P('expert', 'dp'), may hold values from -0.1875 to 0.1875
Outputs:
- grad_tokens: bfloat16 [2048, 7168], P('expert', 'dp')
- grad_gate: bfloat16 [8, 7168, 1024], P('expert', 'dp')
- grad_up: bfloat16 [8, 7168, 1024], P('expert', 'dp')
- grad_down: bfloat16 [8, 1024, 7168], P('expert', None, 'dp')
- grad_shared_gate: float32 [7168, 1024], P('dp', 'expert')
- grad_shared_up: float32 [7168, 1024], P('dp', 'expert')
- grad_shared_down: float32 [1024, 7168], P('expert', 'dp')
The draws below stay inside these ranges and needn't reach their ends.
Inputs may be any that keep to these rules, and one draw needn't show every extreme that they name: `route_ids`: each row names 8 different experts; in each aligned block of 256 rows no expert is named by more than 12 rows, a bound that some block reaches.
All inputs are finite; a program needn't handle non-finite values.
Results may differ from the reference program's by a relative error of at most 0.018.
Values may be sent and summed in bfloat16 or wider, within the bound.
A program may use at most 128 MiB of HBM per device.

```python
import math
import jax
import jax.numpy as jnp
import numpy as np
from jax import lax

D = 7168
HID = 1024
HSH = 1024
ALL_EXP = 256
TOPK = 8
TOK_DEV = 256
EXPERTS = 8
TOKENS = 2048
CAP = 12
N_EXPERT = 8


def block_levels(own_key, shape, split, low, high):
    loudness, own = 1.0, jax.random.fold_in(own_key, 6)
    for dim, parts in split:
        heights = jnp.exp(jax.random.uniform(jax.random.fold_in(own, dim), (parts,), jnp.float32, low / len(split), high / len(split)))
        loudness = loudness * jnp.repeat(heights, shape[dim] // parts).reshape([-1 if axis == dim else 1 for axis in range(len(shape))])
    return loudness


def routed_block(rng, own, number, rows, count, top, limit, skew):
    sequence = jax.random.permutation(rng, count)
    heavy_load, ordinary = shares(count, rows * top, limit, skew, True), shares(count, rows * top, limit, skew, False)
    places = jnp.arange(count)

    def named(lengths, rotation):
        used = int((lengths > 0).sum())
        fixed = max(1, used // 4)
        moved = fixed + (places - fixed + rotation * (used - fixed)) % max(1, count - fixed)
        return jnp.zeros((count,), jnp.int32).at[sequence[jnp.where(places < fixed, places, moved)]].set(jnp.asarray(lengths, jnp.int32))

    lengths = jnp.where(number % 4 == 0, named(heavy_load, number // 4), named(ordinary, number - number // 4 - 1))
    mixed = jax.random.permutation(jax.random.fold_in(own, 3), count)
    donor, receiver = mixed[0:count // 2 * 2:2], mixed[1:count // 2 * 2:2]
    room = jnp.minimum(lengths[donor] - 1, limit - lengths[receiver]) // 2
    room = jnp.where((donor == sequence[0]) | (receiver == sequence[0]) | (lengths[receiver] == 0), 0, jnp.maximum(room, 0))
    moved = jax.random.randint(jax.random.fold_in(own, 4), (count // 2,), 0, 1 << 20) % (room + 1)
    lengths = lengths.at[donor].add(-moved).at[receiver].add(moved)
    members = jnp.searchsorted(jnp.cumsum(lengths), jnp.arange(rows * top), side="right").astype(jnp.int32)
    table = members.reshape(top, rows).T
    table = table[jax.random.permutation(jax.random.fold_in(own, 1), rows)]
    rotation = jax.random.randint(jax.random.fold_in(own, 2), (rows, 1), 0, top)
    return jnp.take_along_axis(table, (jnp.arange(top)[None, :] + rotation) % top, axis=1)


def shares(number_of, total, reach, skew, full):
    weights = [(1 << 20) // math.isqrt(standing ** skew) + 1 for standing in range(1, number_of + 1)]
    largest = reach if full else min(reach, max(-(-total // number_of), total * weights[0] // sum(weights)))
    least = 1 if total - largest >= number_of - 1 else 0
    given, surplus = [largest] + [least] * (number_of - 1), total - largest - least * (number_of - 1)
    while surplus > 0:
        movable = [i for i in range(1, number_of) if given[i] < largest] or [i for i in range(1, number_of) if given[i] < reach]
        mass, budget = sum([weights[i] for i in movable]), surplus
        for i in movable:
            addition = min(reach - given[i], max(1, budget * weights[i] // mass), surplus)
            given[i] = given[i] + addition
            surplus = surplus - addition
    return np.array(given)


def gaussian(rng, dims, deviation, limit, split=(), kind=jnp.bfloat16):
    array = jax.random.normal(rng, dims, jnp.float32) * deviation
    if len(split) > 0:
        array = block_levels(rng, dims, split, -0.22, 0.18) * array
    return jnp.clip(array, min=-limit, max=limit).astype(kind)


def setup_inputs(seed: int = 0) -> dict:
    arg_keys = jax.random.split(jax.random.key(seed), 11)
    tokens = gaussian(arg_keys[0], (TOKENS, D), 1.0, 6.0, ((0, 8), (1, 4)))
    grad_out = gaussian(arg_keys[1], (TOKENS, D), 1.0, 6.0, ((0, 8), (1, 4)))
    route_ids_keys = jax.random.split(jax.random.fold_in(arg_keys[2], 1), TOKENS // TOK_DEV)
    route_ids_turns = jax.random.permutation(jax.random.fold_in(arg_keys[2], 3), TOKENS // TOK_DEV)
    route_ids = jax.vmap(lambda own, number: routed_block(jax.random.fold_in(arg_keys[2], 2), own, number, TOK_DEV, ALL_EXP, TOPK, CAP, 2))(route_ids_keys, route_ids_turns).reshape((TOKENS, TOPK))
    route_gates = jnp.clip(jnp.exp(math.log(1.0) - 2.3025851 * jax.random.uniform(arg_keys[3], (TOKENS, TOPK), jnp.float32) ** block_levels(arg_keys[3], (TOKENS, TOPK), ((0, 8),), -0.2, 0.2)), 0.1, 1.0)
    w_gate = gaussian(arg_keys[4], (EXPERTS, D, HID), D ** -0.5, 0.0625, ((0, 8), (1, 4)))
    w_up = gaussian(arg_keys[5], (EXPERTS, D, HID), D ** -0.5, 0.0625, ((0, 8), (1, 4)))
    w_down = gaussian(arg_keys[6], (EXPERTS, HID, D), HID ** -0.5, 0.1875, ((0, 8), (2, 4)))
    shared_gate = gaussian(arg_keys[7], (D, HSH), D ** -0.5, 0.0625, ((0, 4), (1, 8)))
    shared_up = gaussian(arg_keys[8], (D, HSH), D ** -0.5, 0.0625, ((0, 4), (1, 8)))
    shared_down = gaussian(arg_keys[9], (HSH, D), HSH ** -0.5, 0.1875, ((0, 8), (1, 4)))
    return dict(tokens=tokens, grad_out=grad_out, route_ids=route_ids, route_gates=route_gates, w_gate=w_gate, w_up=w_up, w_down=w_down, shared_gate=shared_gate, shared_up=shared_up, shared_down=shared_down)


def silu_parts(pre):
    sigmoid_val = jax.nn.sigmoid(pre)
    return pre * sigmoid_val, sigmoid_val * (1.0 + pre * (1.0 - sigmoid_val))


def contract_rows(left, right):
    return lax.dot_general(left, right, (((0,), (0,)), ((), ())), preferred_element_type=jnp.float32)


def contract_cols(left, right):
    return lax.dot_general(left, right, (((1,), (1,)), ((), ())), preferred_element_type=jnp.float32)


def expert_terms(rows_in, rows_grad, weight_gate, weight_up, weight_down):
    pre_gate = jnp.dot(rows_in, weight_gate, preferred_element_type=jnp.float32)
    pre_up = jnp.dot(rows_in, weight_up, preferred_element_type=jnp.float32)
    grad_act = contract_cols(rows_grad, weight_down)
    silu_val, silu_slope = silu_parts(pre_gate)
    activated = (silu_val * pre_up).astype(jnp.bfloat16)
    grad_gate_pre = (grad_act * pre_up * silu_slope).astype(jnp.bfloat16)
    grad_up_pre = (grad_act * silu_val).astype(jnp.bfloat16)
    back = contract_cols(grad_gate_pre, weight_gate) + contract_cols(grad_up_pre, weight_up)
    return (contract_rows(rows_in, grad_gate_pre), contract_rows(rows_in, grad_up_pre),
            contract_rows(activated, rows_grad), back)


def settle(value):
    return lax.optimization_barrier(value.astype(jnp.bfloat16)).astype(jnp.float32)


def reference(tokens, grad_out, route_ids, route_gates, w_gate, w_up, w_down, shared_gate, shared_up, shared_down):
    grad_scale = 1.0 / N_EXPERT
    row_count = N_EXPERT * CAP
    order_base = jnp.arange(TOKENS, dtype=jnp.int32)

    def one_expert(carry, expert_id):
        matches = route_ids == expert_id
        chosen = jnp.any(matches, axis=1)
        gate_total = jnp.sum(jnp.where(matches, route_gates, jnp.zeros_like(route_gates)), axis=1)
        sort_key = jnp.where(chosen, 0, TOKENS).astype(jnp.int32) + order_base
        picked = jnp.argsort(sort_key)[:row_count].astype(jnp.int32)
        rows_in = tokens[picked]
        rows_grad = (gate_total[picked][:, None] * grad_out[picked].astype(jnp.float32)).astype(jnp.bfloat16)
        part_gate, part_up, part_down, back = expert_terms(rows_in, rows_grad, w_gate[expert_id], w_up[expert_id], w_down[expert_id])
        carry = carry.at[picked].add(settle(back))
        return carry, ((part_gate * grad_scale).astype(jnp.bfloat16), (part_up * grad_scale).astype(jnp.bfloat16),
                       (part_down * grad_scale).astype(jnp.bfloat16))

    routed, (grad_gate, grad_up, grad_down) = lax.scan(
        one_expert, jnp.zeros((TOKENS, D), jnp.float32), jnp.arange(EXPERTS, dtype=jnp.int32))

    groups_in = tokens.reshape(N_EXPERT, TOK_DEV, D)
    groups_grad = grad_out.reshape(N_EXPERT, TOK_DEV, D)

    def one_group(carry, pair):
        rows_in, rows_grad = pair
        part_gate, part_up, part_down, back = expert_terms(rows_in, rows_grad, shared_gate, shared_up, shared_down)
        return (carry[0] + part_gate, carry[1] + part_up, carry[2] + part_down), back

    start = (jnp.zeros((D, HSH), jnp.float32), jnp.zeros((D, HSH), jnp.float32), jnp.zeros((HSH, D), jnp.float32))
    (sum_gate, sum_up, sum_down), shared_back = lax.scan(one_group, start, (groups_in, groups_grad))
    grad_tokens = (shared_back.reshape(TOKENS, D) + routed).astype(jnp.bfloat16)
    return (grad_tokens, grad_gate, grad_up, grad_down,
            sum_gate * grad_scale, sum_up * grad_scale, sum_down * grad_scale)
```

```python
import jax
import jax.numpy as jnp
from jax import lax
from jax.sharding import PartitionSpec as P

CAP = 12


def silu_parts(pre):
    sigmoid_val = jax.nn.sigmoid(pre)
    return (pre * sigmoid_val, sigmoid_val * (1.0 + pre * (1.0 - sigmoid_val)))


def contract_rows(left, right):
    return lax.dot_general(
        left, right, (((0,), (0,)), ((), ())), preferred_element_type=jnp.float32
    )


def contract_cols(left, right):
    return lax.dot_general(
        left, right, (((1,), (1,)), ((), ())), preferred_element_type=jnp.float32
    )


def hidden_products(part_gate, part_up, part_act):
    silu_val, silu_slope = silu_parts(part_gate)
    activated = (silu_val * part_up).astype(jnp.bfloat16)
    grad_gate_pre = (part_act * part_up * silu_slope).astype(jnp.bfloat16)
    grad_up_pre = (part_act * silu_val).astype(jnp.bfloat16)
    return (activated, grad_gate_pre, grad_up_pre)


def axis_groups(n_exp):
    inner = 1
    while inner * inner * 4 <= n_exp:
        inner *= 2
    outer = n_exp // inner
    near = [[o * inner + i for i in range(inner)] for o in range(outer)]
    far = [[o * inner + i for o in range(outer)] for i in range(inner)]
    return near, far


def partial_products(rows_in, rows_grad, weight_gate, weight_up, weight_down):
    part_gate = jnp.dot(rows_in, weight_gate, preferred_element_type=jnp.float32)
    part_up = jnp.dot(rows_in, weight_up, preferred_element_type=jnp.float32)
    part_act = contract_cols(rows_grad, weight_down)
    return tuple(part.astype(jnp.bfloat16) for part in (part_gate, part_up, part_act))


def expert_grads(sums, rows_in, rows_grad, weight_gate, weight_up):
    pre_gate, pre_up, grad_act = (total.astype(jnp.float32) for total in sums)
    activated, grad_gate_pre, grad_up_pre = hidden_products(pre_gate, pre_up, grad_act)
    back = contract_cols(grad_gate_pre, weight_gate) + contract_cols(grad_up_pre, weight_up)
    return (
        contract_rows(rows_in, grad_gate_pre),
        contract_rows(rows_in, grad_up_pre),
        contract_rows(activated, rows_grad),
        back.astype(jnp.bfloat16),
    )


def shards(
    tokens,
    grad_out,
    route_ids,
    route_gates,
    w_gate,
    w_up,
    w_down,
    shared_gate,
    shared_up,
    shared_down,
):
    n_exp = lax.axis_size("expert")
    capacity = CAP
    grad_scale = 1.0 / n_exp
    targets = jnp.arange(n_exp, dtype=jnp.int32)
    matches = route_ids[:, :, None] == targets[None, None, :]
    chosen = jnp.any(matches, axis=1).astype(jnp.int32)
    gate_total = jnp.sum(jnp.where(matches, route_gates[:, :, None], 0.0), axis=1)
    slot_rank = jnp.cumsum(chosen, axis=0) - 1
    slot_ids = jnp.arange(capacity, dtype=jnp.int32)
    placement = (chosen[:, :, None] == 1) & (slot_rank[:, :, None] == slot_ids[None, None, :])
    place_bf = placement.astype(jnp.bfloat16)
    send_in = jnp.einsum(
        "tec,td->ecd", place_bf, tokens, preferred_element_type=jnp.float32
    ).astype(jnp.bfloat16)
    slot_gate = jnp.einsum("tec,te->ec", placement.astype(jnp.float32), gate_total)
    picked_grad = jnp.einsum("tec,td->ecd", place_bf, grad_out, preferred_element_type=jnp.float32)
    send_grad = (slot_gate[:, :, None] * picked_grad).astype(jnp.bfloat16)
    width_dev = tokens.shape[1]
    near, far = axis_groups(n_exp)

    def scatter(part, groups, dim):
        return lax.psum_scatter(
            part, "expert", scatter_dimension=dim, axis_index_groups=groups, tiled=True
        )

    def gather(part, groups, dim):
        return lax.all_gather(part, "expert", axis=dim, axis_index_groups=groups, tiled=True)

    recv = lax.all_to_all(
        jnp.concatenate([send_in, send_grad], axis=1), "expert", split_axis=0, concat_axis=0, tiled=True
    )
    rows_in = recv[:, :capacity].reshape(n_exp * capacity, width_dev)
    rows_grad = recv[:, capacity:].reshape(n_exp * capacity, width_dev)
    all_in, all_grad = gather(tokens, near, 0), gather(grad_out, near, 0)
    far_gate, far_up, far_down = (
        gather(shared_gate, far, 1), gather(shared_up, far, 1), gather(shared_down, far, 0)
    )
    routed_parts = partial_products(rows_in, rows_grad, w_gate[0], w_up[0], w_down[0])
    shared_parts = partial_products(all_in, all_grad, far_gate, far_up, far_down)
    sums = lax.psum(routed_parts + shared_parts, "dp")
    own_gate, own_up, own_down, shared_back = expert_grads(
        sums[3:], all_in, all_grad, far_gate, far_up
    )
    part_gate, part_up, part_down, back = expert_grads(
        sums[:3], rows_in, rows_grad, w_gate[0], w_up[0]
    )
    sum_gate = scatter(own_gate.astype(jnp.bfloat16), far, 1)
    sum_up = scatter(own_up.astype(jnp.bfloat16), far, 1)
    sum_down = scatter(own_down.astype(jnp.bfloat16), far, 0)
    sum_back = scatter(shared_back, near, 0)
    back_rows = lax.all_to_all(
        back.reshape(n_exp, capacity, width_dev), "expert", split_axis=0, concat_axis=0, tiled=True
    )
    routed = jnp.einsum("tec,ecd->td", place_bf, back_rows, preferred_element_type=jnp.float32)
    return (
        (sum_back.astype(jnp.float32) + routed).astype(jnp.bfloat16),
        (part_gate * grad_scale).astype(jnp.bfloat16)[None],
        (part_up * grad_scale).astype(jnp.bfloat16)[None],
        (part_down * grad_scale).astype(jnp.bfloat16)[None],
        sum_gate.astype(jnp.float32) * grad_scale,
        sum_up.astype(jnp.float32) * grad_scale,
        sum_down.astype(jnp.float32) * grad_scale,
    )


def solution(mesh):
    in_specs = (
        P("expert", "dp"),
        P("expert", "dp"),
        P("expert", None),
        P("expert", None),
        P("expert", "dp", None),
        P("expert", "dp", None),
        P("expert", None, "dp"),
        P("dp", "expert"),
        P("dp", "expert"),
        P("expert", "dp"),
    )
    out_specs = (
        P("expert", "dp"),
        P("expert", "dp", None),
        P("expert", "dp", None),
        P("expert", None, "dp"),
        P("dp", "expert"),
        P("dp", "expert"),
        P("expert", "dp"),
    )
    return jax.shard_map(shards, mesh=mesh, in_specs=in_specs, out_specs=out_specs, check_vma=False)
```

```python
import functools

import jax
import jax.numpy as jnp
from jax import lax
from jax.experimental import pallas as pl
from jax.experimental.pallas import tpu as pltpu
from jax.sharding import PartitionSpec as P

CAP = 12
SLOT = 16
NEAR = 4
MESH = pl.DeviceIdType.MESH
ANY = pl.BlockSpec(memory_space=pl.ANY)
VMEM = pl.BlockSpec(memory_space=pltpu.VMEM)


def silu_parts(pre):
    sigmoid_val = jax.nn.sigmoid(pre)
    return (pre * sigmoid_val, sigmoid_val * (1.0 + pre * (1.0 - sigmoid_val)))


def contract_rows(left, right):
    return lax.dot_general(
        left, right, (((0,), (0,)), ((), ())), preferred_element_type=jnp.float32
    )


def contract_cols(left, right):
    return lax.dot_general(
        left, right, (((1,), (1,)), ((), ())), preferred_element_type=jnp.float32
    )


def hidden_products(part_gate, part_up, part_act):
    silu_val, silu_slope = silu_parts(part_gate)
    activated = (silu_val * part_up).astype(jnp.bfloat16)
    grad_gate_pre = (part_act * part_up * silu_slope).astype(jnp.bfloat16)
    grad_up_pre = (part_act * silu_val).astype(jnp.bfloat16)
    return (activated, grad_gate_pre, grad_up_pre)


def greet(peers):
    barrier = pltpu.get_barrier_semaphore()
    for peer in peers:
        pl.semaphore_signal(barrier, inc=1, device_id=peer, device_id_type=MESH)
    pl.semaphore_wait(barrier, len(peers))


def remote(src, dst, sems, k, peer):
    return pltpu.make_async_remote_copy(
        src_ref=src,
        dst_ref=dst,
        send_sem=sems[0].at[k],
        recv_sem=sems[1].at[k],
        device_id=peer,
        device_id_type=MESH,
    )


def expert_peers(n_exp):
    dp, me = lax.axis_index("dp"), lax.axis_index("expert")
    far, near = me // NEAR, me % NEAR
    high, low = near // 2, near % 2
    n_far = n_exp // NEAR
    base = far * NEAR
    across = (dp, base + (1 - high) * 2 + low)
    beside = (dp, base + high * 2 + 1 - low)
    corner = (dp, base + (1 - high) * 2 + 1 - low)
    distant = [(dp, lax.rem(far + k, n_far) * NEAR + near) for k in range(1, n_far)]
    every = [(dp, lax.rem(me + k, n_exp)) for k in range(1, n_exp)]
    return me, near, far, across, beside, corner, distant, every


def gather_kernel(n_exp, *refs):
    tokens, grads, *weights = refs[:5]
    sends = refs[5]
    all_tokens, all_grads, *all_weights = refs[6:11]
    recv = refs[11]
    near_sems, far_sems, route_sems = refs[12:14], refs[14:16], refs[16:18]
    own_sem = refs[18]
    me, near, far, across, beside, corner, distant, every = expert_peers(n_exp)
    greet(every)
    pairs = ((tokens, all_tokens), (grads, all_grads))
    copies, relays = [], []
    for k, (src, dst) in enumerate(pairs):
        relays.append(remote(src, dst.at[near], near_sems, 3 * k, across))
        copies.append(remote(src, dst.at[near], near_sems, 3 * k + 1, beside))
        relays[-1].start()
        copies[-1].start()
    for k, peer in enumerate(every):
        copies.append(remote(sends.at[peer[1]], recv.at[me], route_sems, k, peer))
        copies[-1].start()
    for k, peer in enumerate(distant):
        for w in range(3):
            copies.append(remote(weights[w], all_weights[w].at[far], far_sems, 3 * k + w, peer))
            copies[-1].start()
    own = [
        pltpu.make_async_copy(src, dst, own_sem.at[k])
        for k, (src, dst) in enumerate(
            [(src, dst.at[near]) for src, dst in pairs]
            + [(weights[w], all_weights[w].at[far]) for w in range(3)]
            + [(sends.at[me], recv.at[me])]
        )
    ]
    for copy in own:
        copy.start()
    other = lax.rem(near + 2, NEAR)
    for k, (_, dst) in enumerate(pairs):
        relays[k].wait_recv()
        copies.append(remote(dst.at[other], dst.at[other], near_sems, 3 * k + 2, beside))
        copies[-1].start()
    for copy in relays:
        copy.wait_send()
    for copy in own:
        copy.wait()
    for copy in copies:
        copy.wait()


def gather_call(n_exp, *args):
    n_far = n_exp // NEAR
    shapes = [(NEAR,) + a.shape for a in args[:2]] + [(n_far,) + a.shape for a in args[2:5]]
    shapes.append(args[5].shape)
    counts = (6, 6, 3 * (n_far - 1), 3 * (n_far - 1), n_exp - 1, n_exp - 1, 6)
    return pl.pallas_call(
        functools.partial(gather_kernel, n_exp),
        out_shape=[jax.ShapeDtypeStruct(shape, jnp.bfloat16) for shape in shapes],
        in_specs=[ANY] * 6,
        out_specs=[ANY] * 6,
        scratch_shapes=[pltpu.SemaphoreType.DMA((count,)) for count in counts],
        compiler_params=pltpu.CompilerParams(collective_id=1, has_side_effects=True),
    )(*args)


def scatter_kernel(n_exp, *refs):
    back, *parts = refs[:4]
    sends = refs[4]
    got_back, *got_parts = refs[5:9]
    recv = refs[9]
    near_sems, far_sems, route_sems = refs[10:12], refs[12:14], refs[14:16]
    own_sem = refs[16]
    me, near, far, across, beside, corner, distant, every = expert_peers(n_exp)
    greet(every)
    copies = []
    for k, peer in enumerate(distant):
        for w in range(3):
            copies.append(
                remote(parts[w].at[peer[1] // NEAR], got_parts[w].at[far], far_sems, 3 * k + w, peer)
            )
    for k, peer in enumerate((corner, across, beside)):
        copies.append(remote(back.at[lax.rem(peer[1], NEAR)], got_back.at[near], near_sems, k, peer))
    for k, peer in enumerate(every):
        copies.append(remote(sends.at[peer[1]], recv.at[me], route_sems, k, peer))
    own = [
        pltpu.make_async_copy(src, dst, own_sem.at[k])
        for k, (src, dst) in enumerate(
            [(back.at[near], got_back.at[near])]
            + [(parts[w].at[far], got_parts[w].at[far]) for w in range(3)]
            + [(sends.at[me], recv.at[me])]
        )
    ]
    for copy in copies + own:
        copy.start()
    for copy in own + copies:
        copy.wait()


def scatter_call(n_exp, *args):
    n_far = n_exp // NEAR
    counts = (3, 3, 3 * (n_far - 1), 3 * (n_far - 1), n_exp - 1, n_exp - 1, 5)
    return pl.pallas_call(
        functools.partial(scatter_kernel, n_exp),
        out_shape=[jax.ShapeDtypeStruct(a.shape, jnp.bfloat16) for a in args],
        in_specs=[ANY] * 5,
        out_specs=[ANY] * 5,
        scratch_shapes=[pltpu.SemaphoreType.DMA((count,)) for count in counts],
        compiler_params=pltpu.CompilerParams(collective_id=2, has_side_effects=True),
    )(*args)


def hidden_kernel(n_dp, *refs):
    parts, outs = refs[:2], refs[2:4]
    met, held, far = refs[4:6], refs[6:8], refs[8:10]
    meet_sems, far_sems, give_sems = refs[10:12], refs[12:14], refs[14:16]
    dp, expert = lax.axis_index("dp"), lax.axis_index("expert")
    chip, core = dp // 2, dp % 2
    chips = n_dp // 2
    twin = (chip * 2 + 1 - core, expert)
    peers = [(lax.rem(chip + k, chips) * 2 + core, expert) for k in range(1, chips)]
    greet([twin] + peers)
    meets = [remote(parts[a].at[:, 1 - core], met[a], meet_sems, a, twin) for a in range(2)]
    for copy in meets:
        copy.start()
    copies = []
    for a in range(2):
        rows = 64 if met[a].shape[1] % 64 == 0 else SLOT
        meets[a].wait()

        @pl.loop(0, met[a].shape[1] // rows)
        def _(step):
            at = pl.ds(pl.multiple_of(step * rows, rows), rows)
            for w in range(3):
                held[a][w, at] = (
                    parts[a][w, core, at].astype(jnp.float32) + met[a][w, at].astype(jnp.float32)
                ).astype(jnp.bfloat16)

        copies.append(
            [
                remote(held[a], far[a].at[k], far_sems, a * (chips - 1) + k, peer)
                for k, peer in enumerate(peers)
            ]
        )
        for copy in copies[-1]:
            copy.start()
    gives = []
    for a in range(2):
        rows = 64 if met[a].shape[1] % 64 == 0 else SLOT
        for copy in copies[a]:
            copy.wait()

        @pl.loop(0, met[a].shape[1] // rows)
        def _(step):
            at = pl.ds(pl.multiple_of(step * rows, rows), rows)
            totals = []
            for w in range(3):
                total = held[a][w, at].astype(jnp.float32)
                for k in range(chips - 1):
                    total = total + far[a][k, w, at].astype(jnp.float32)
                totals.append(total)
            for w, value in enumerate(hidden_products(*totals)):
                outs[a][w, core, at] = value

        gives.append(remote(outs[a].at[:, core], outs[a].at[:, core], give_sems, a, twin))
        gives[-1].start()
    for copy in gives:
        copy.wait()


def hidden_call(n_dp, *args):
    chips = n_dp // 2
    halves = [(3,) + a.shape[2:] for a in args]
    return pl.pallas_call(
        functools.partial(hidden_kernel, n_dp),
        out_shape=[jax.ShapeDtypeStruct(a.shape, jnp.bfloat16) for a in args],
        in_specs=[VMEM] * 2,
        out_specs=[VMEM] * 2,
        scratch_shapes=[pltpu.VMEM(shape, jnp.bfloat16) for shape in halves * 2]
        + [pltpu.VMEM((chips - 1,) + shape, jnp.bfloat16) for shape in halves]
        + [
            pltpu.SemaphoreType.DMA((count,))
            for count in (2, 2, 2 * (chips - 1), 2 * (chips - 1), 2, 2)
        ],
        compiler_params=pltpu.CompilerParams(
            collective_id=3, has_side_effects=True, vmem_limit_bytes=40 * 2**20
        ),
    )(*args)


def partial_products(rows_in, rows_grad, weight_gate, weight_up, weight_down):
    part_gate = jnp.dot(rows_in, weight_gate, preferred_element_type=jnp.float32)
    part_up = jnp.dot(rows_in, weight_up, preferred_element_type=jnp.float32)
    part_act = contract_cols(rows_grad, weight_down)
    parts = jnp.stack([part.astype(jnp.bfloat16) for part in (part_gate, part_up, part_act)])
    rows, width = part_gate.shape
    return parts.reshape(3, 2, rows // 2, width)


def shards(
    tokens,
    grad_out,
    route_ids,
    route_gates,
    w_gate,
    w_up,
    w_down,
    shared_gate,
    shared_up,
    shared_down,
):
    n_exp = lax.axis_size("expert")
    capacity = SLOT
    grad_scale = 1.0 / n_exp
    targets = jnp.arange(n_exp, dtype=jnp.int32)
    matches = route_ids[:, :, None] == targets[None, None, :]
    chosen = jnp.any(matches, axis=1).astype(jnp.int32)
    gate_total = jnp.sum(jnp.where(matches, route_gates[:, :, None], 0.0), axis=1)
    slot_rank = jnp.cumsum(chosen, axis=0) - 1
    slot_ids = jnp.arange(capacity, dtype=jnp.int32)
    placement = (chosen[:, :, None] == 1) & (slot_rank[:, :, None] == slot_ids[None, None, :])
    place_bf = placement.astype(jnp.bfloat16)
    picked_in = jnp.einsum("tec,td->ecd", place_bf, tokens, preferred_element_type=jnp.float32)
    slot_gate = jnp.einsum("tec,te->ec", placement.astype(jnp.float32), gate_total)
    picked_grad = jnp.einsum("tec,td->ecd", place_bf, grad_out, preferred_element_type=jnp.float32)
    picked = jnp.stack([picked_in, slot_gate[:, :, None] * picked_grad], axis=1).astype(jnp.bfloat16)
    width_dev = tokens.shape[1]
    sends = picked.reshape(n_exp, 2 * capacity, width_dev)
    all_in, all_grad, far_gate, far_up, far_down, recv = gather_call(
        n_exp, tokens, grad_out, shared_gate, shared_up, shared_down, sends
    )
    n_far = n_exp // NEAR
    width_sh = shared_gate.shape[1]
    all_in, all_grad = all_in.reshape(-1, width_dev), all_grad.reshape(-1, width_dev)
    far_gate = jnp.concatenate([far_gate[k] for k in range(n_far)], axis=1)
    far_up = jnp.concatenate([far_up[k] for k in range(n_far)], axis=1)
    far_down = far_down.reshape(-1, width_dev)
    recv = recv.reshape(n_exp, 2, capacity, width_dev)
    rows_in = recv[:, 0].reshape(n_exp * capacity, width_dev)
    rows_grad = recv[:, 1].reshape(n_exp * capacity, width_dev)
    shared_acts, routed_acts = hidden_call(
        lax.axis_size("dp"),
        partial_products(all_in, all_grad, far_gate, far_up, far_down),
        partial_products(rows_in, rows_grad, w_gate[0], w_up[0], w_down[0]),
    )
    act, grad_gate_pre, grad_up_pre = (
        shared_acts[w].reshape(-1, n_far * width_sh) for w in range(3)
    )
    back = contract_cols(grad_gate_pre, far_gate) + contract_cols(grad_up_pre, far_up)

    def own_columns(grad_pre):
        return jnp.stack(
            [
                contract_rows(all_in, grad_pre[:, k * width_sh : (k + 1) * width_sh])
                for k in range(n_far)
            ]
        ).astype(jnp.bfloat16)

    routed_act, routed_gate, routed_up = (
        routed_acts[w].reshape(n_exp * capacity, -1) for w in range(3)
    )
    route_back = contract_cols(routed_gate, w_gate[0]) + contract_cols(routed_up, w_up[0])
    got_back, got_gate, got_up, got_down, back_rows = scatter_call(
        n_exp,
        back.astype(jnp.bfloat16).reshape(NEAR, -1, width_dev),
        own_columns(grad_gate_pre),
        own_columns(grad_up_pre),
        contract_rows(act, all_grad).astype(jnp.bfloat16).reshape(n_far, width_sh, width_dev),
        route_back.astype(jnp.bfloat16).reshape(n_exp, capacity, width_dev),
    )

    def total(parts):
        return jnp.sum(parts.astype(jnp.float32), axis=0)

    routed = jnp.einsum("tec,ecd->td", place_bf, back_rows, preferred_element_type=jnp.float32)
    return (
        (total(got_back) + routed).astype(jnp.bfloat16),
        (contract_rows(rows_in, routed_gate) * grad_scale).astype(jnp.bfloat16)[None],
        (contract_rows(rows_in, routed_up) * grad_scale).astype(jnp.bfloat16)[None],
        (contract_rows(routed_act, rows_grad) * grad_scale).astype(jnp.bfloat16)[None],
        total(got_gate) * grad_scale,
        total(got_up) * grad_scale,
        total(got_down) * grad_scale,
    )


def solution(mesh):
    in_specs = (
        P("expert", "dp"),
        P("expert", "dp"),
        P("expert", None),
        P("expert", None),
        P("expert", "dp", None),
        P("expert", "dp", None),
        P("expert", None, "dp"),
        P("dp", "expert"),
        P("dp", "expert"),
        P("expert", "dp"),
    )
    out_specs = (
        P("expert", "dp"),
        P("expert", "dp", None),
        P("expert", "dp", None),
        P("expert", None, "dp"),
        P("dp", "expert"),
        P("dp", "expert"),
        P("expert", "dp"),
    )
    return jax.shard_map(shards, mesh=mesh, in_specs=in_specs, out_specs=out_specs, check_vma=False)
```

```python
import functools

import jax
import jax.numpy as jnp
from jax import lax
from jax.experimental import pallas as pl
from jax.experimental.pallas import tpu as pltpu
from jax.sharding import PartitionSpec as P

CAP = 12
SLOT = 16
NEAR = 4
CHUNKS = 4
MESH = pl.DeviceIdType.MESH
ANY = pl.BlockSpec(memory_space=pl.ANY)
VMEM = pl.BlockSpec(memory_space=pltpu.VMEM)


def silu_parts(pre):
    sigmoid_val = jax.nn.sigmoid(pre)
    return (pre * sigmoid_val, sigmoid_val * (1.0 + pre * (1.0 - sigmoid_val)))


def contract_rows(left, right):
    return lax.dot_general(
        left, right, (((0,), (0,)), ((), ())), preferred_element_type=jnp.float32
    )


def contract_cols(left, right):
    return lax.dot_general(
        left, right, (((1,), (1,)), ((), ())), preferred_element_type=jnp.float32
    )


def hidden_products(part_gate, part_up, part_act):
    silu_val, silu_slope = silu_parts(part_gate)
    activated = (silu_val * part_up).astype(jnp.bfloat16)
    grad_gate_pre = (part_act * part_up * silu_slope).astype(jnp.bfloat16)
    grad_up_pre = (part_act * silu_val).astype(jnp.bfloat16)
    return (activated, grad_gate_pre, grad_up_pre)


def greet(peers):
    barrier = pltpu.get_barrier_semaphore()
    for peer in peers:
        pl.semaphore_signal(barrier, inc=1, device_id=peer, device_id_type=MESH)
    pl.semaphore_wait(barrier, len(peers))


def remote(src, dst, sems, k, peer):
    return pltpu.make_async_remote_copy(
        src_ref=src,
        dst_ref=dst,
        send_sem=sems[0].at[k],
        recv_sem=sems[1].at[k],
        device_id=peer,
        device_id_type=MESH,
    )


def expert_peers(n_exp):
    dp, me = lax.axis_index("dp"), lax.axis_index("expert")
    far, near = me // NEAR, me % NEAR
    high, low = near // 2, near % 2
    n_far = n_exp // NEAR
    base = far * NEAR
    across = (dp, base + (1 - high) * 2 + low)
    beside = (dp, base + high * 2 + 1 - low)
    corner = (dp, base + (1 - high) * 2 + 1 - low)
    distant = [(dp, lax.rem(far + k, n_far) * NEAR + near) for k in range(1, n_far)]
    every = [(dp, lax.rem(me + k, n_exp)) for k in range(1, n_exp)]
    return me, near, far, across, beside, corner, distant, every


def gather_kernel(n_exp, *refs):
    tokens, grads, *weights = refs[:5]
    sends = refs[5]
    all_tokens, all_grads, *all_weights = refs[6:11]
    recv = refs[11]
    near_sems, far_sems, route_sems = refs[12:14], refs[14:16], refs[16:18]
    own_sem = refs[18]
    me, near, far, across, beside, corner, distant, every = expert_peers(n_exp)
    greet(every)
    pairs = ((tokens, all_tokens), (grads, all_grads))
    rows = tokens.shape[0] // CHUNKS
    copies, relays = [], []
    for k, (src, dst) in enumerate(pairs):
        for c in range(CHUNKS):
            at, sem = pl.ds(c * rows, rows), 3 * (k * CHUNKS + c)
            relays.append(remote(src.at[at], dst.at[near, at], near_sems, sem, across))
            copies.append(remote(src.at[at], dst.at[near, at], near_sems, sem + 1, beside))
            relays[-1].start()
            copies[-1].start()
        for p, peer in enumerate(distant):
            for w in ((0, 1), (2,))[k]:
                copies.append(remote(weights[w], all_weights[w].at[far], far_sems, 3 * p + w, peer))
                copies[-1].start()
    for k, peer in enumerate(every):
        copies.append(remote(sends.at[peer[1]], recv.at[me], route_sems, k, peer))
        copies[-1].start()
    own = [
        pltpu.make_async_copy(src, dst, own_sem.at[k])
        for k, (src, dst) in enumerate(
            [(src, dst.at[near]) for src, dst in pairs]
            + [(weights[w], all_weights[w].at[far]) for w in range(3)]
            + [(sends.at[me], recv.at[me])]
        )
    ]
    for copy in own:
        copy.start()
    other = lax.rem(near + 2, NEAR)
    for k, (_, dst) in enumerate(pairs):
        for c in range(CHUNKS):
            block, sem = dst.at[other, pl.ds(c * rows, rows)], 3 * (k * CHUNKS + c)
            relays[k * CHUNKS + c].wait_recv()
            copies.append(remote(block, block, near_sems, sem + 2, beside))
            copies[-1].start()
    for copy in relays:
        copy.wait_send()
    for copy in own:
        copy.wait()
    for copy in copies:
        copy.wait()


def gather_call(n_exp, *args):
    n_far = n_exp // NEAR
    shapes = [(NEAR,) + a.shape for a in args[:2]] + [(n_far,) + a.shape for a in args[2:5]]
    shapes.append(args[5].shape)
    counts = (6 * CHUNKS, 6 * CHUNKS, 3 * (n_far - 1), 3 * (n_far - 1), n_exp - 1, n_exp - 1, 6)
    return pl.pallas_call(
        functools.partial(gather_kernel, n_exp),
        out_shape=[jax.ShapeDtypeStruct(shape, jnp.bfloat16) for shape in shapes],
        in_specs=[ANY] * 6,
        out_specs=[ANY] * 6,
        scratch_shapes=[pltpu.SemaphoreType.DMA((count,)) for count in counts],
        compiler_params=pltpu.CompilerParams(collective_id=1, has_side_effects=True),
    )(*args)


def hidden_kernel(n_dp, *refs):
    parts, outs = refs[:2], refs[2:4]
    met, held, far = refs[4:6], refs[6:8], refs[8:10]
    meet_sems, far_sems, give_sems = refs[10:12], refs[12:14], refs[14:16]
    dp, expert = lax.axis_index("dp"), lax.axis_index("expert")
    chip, core = dp // 2, dp % 2
    chips = n_dp // 2
    twin = (chip * 2 + 1 - core, expert)
    peers = [(lax.rem(chip + k, chips) * 2 + core, expert) for k in range(1, chips)]
    greet([twin] + peers)
    meets = [remote(parts[a].at[:, 1 - core], met[a], meet_sems, a, twin) for a in range(2)]
    for copy in meets:
        copy.start()
    copies = []
    for a in range(2):
        rows = 64 if met[a].shape[1] % 64 == 0 else SLOT
        meets[a].wait()

        @pl.loop(0, met[a].shape[1] // rows)
        def _(step):
            at = pl.ds(pl.multiple_of(step * rows, rows), rows)
            for w in range(3):
                held[a][w, at] = (
                    parts[a][w, core, at].astype(jnp.float32) + met[a][w, at].astype(jnp.float32)
                ).astype(jnp.bfloat16)

        copies.append(
            [
                remote(held[a], far[a].at[k], far_sems, a * (chips - 1) + k, peer)
                for k, peer in enumerate(peers)
            ]
        )
        for copy in copies[-1]:
            copy.start()
    gives = []
    for a in range(2):
        rows = 64 if met[a].shape[1] % 64 == 0 else SLOT
        for copy in copies[a]:
            copy.wait()

        @pl.loop(0, met[a].shape[1] // rows)
        def _(step):
            at = pl.ds(pl.multiple_of(step * rows, rows), rows)
            totals = []
            for w in range(3):
                total = held[a][w, at].astype(jnp.float32)
                for k in range(chips - 1):
                    total = total + far[a][k, w, at].astype(jnp.float32)
                totals.append(total)
            for w, value in enumerate(hidden_products(*totals)):
                outs[a][w, core, at] = value

        gives.append(remote(outs[a].at[:, core], outs[a].at[:, core], give_sems, a, twin))
        gives[-1].start()
    for copy in gives:
        copy.wait()


def hidden_call(n_dp, *args):
    chips = n_dp // 2
    halves = [(3,) + a.shape[2:] for a in args]
    return pl.pallas_call(
        functools.partial(hidden_kernel, n_dp),
        out_shape=[jax.ShapeDtypeStruct(a.shape, jnp.bfloat16) for a in args],
        in_specs=[VMEM] * 2,
        out_specs=[VMEM] * 2,
        scratch_shapes=[pltpu.VMEM(shape, jnp.bfloat16) for shape in halves * 2]
        + [pltpu.VMEM((chips - 1,) + shape, jnp.bfloat16) for shape in halves]
        + [
            pltpu.SemaphoreType.DMA((count,))
            for count in (2, 2, 2 * (chips - 1), 2 * (chips - 1), 2, 2)
        ],
        compiler_params=pltpu.CompilerParams(
            collective_id=3, has_side_effects=True, vmem_limit_bytes=40 * 2**20
        ),
    )(*args)


def partial_products(rows_in, rows_grad, weight_gate, weight_up, weight_down):
    part_gate = jnp.dot(rows_in, weight_gate, preferred_element_type=jnp.float32)
    part_up = jnp.dot(rows_in, weight_up, preferred_element_type=jnp.float32)
    part_act = contract_cols(rows_grad, weight_down)
    parts = jnp.stack([part.astype(jnp.bfloat16) for part in (part_gate, part_up, part_act)])
    rows, width = part_gate.shape
    return parts.reshape(3, 2, rows // 2, width)


def shards(
    tokens,
    grad_out,
    route_ids,
    route_gates,
    w_gate,
    w_up,
    w_down,
    shared_gate,
    shared_up,
    shared_down,
):
    n_exp = lax.axis_size("expert")
    capacity = SLOT
    grad_scale = 1.0 / n_exp
    targets = jnp.arange(n_exp, dtype=jnp.int32)
    matches = route_ids[:, :, None] == targets[None, None, :]
    chosen = jnp.any(matches, axis=1).astype(jnp.int32)
    gate_total = jnp.sum(jnp.where(matches, route_gates[:, :, None], 0.0), axis=1)
    slot_rank = jnp.cumsum(chosen, axis=0) - 1
    slot_ids = jnp.arange(capacity, dtype=jnp.int32)
    placement = (chosen[:, :, None] == 1) & (slot_rank[:, :, None] == slot_ids[None, None, :])
    place_bf = placement.astype(jnp.bfloat16)
    picked_in = jnp.einsum("tec,td->ecd", place_bf, tokens, preferred_element_type=jnp.float32)
    slot_gate = jnp.einsum("tec,te->ec", placement.astype(jnp.float32), gate_total)
    picked_grad = jnp.einsum("tec,td->ecd", place_bf, grad_out, preferred_element_type=jnp.float32)
    picked = jnp.stack([picked_in, slot_gate[:, :, None] * picked_grad], axis=1).astype(jnp.bfloat16)
    width_dev = tokens.shape[1]
    sends = picked.reshape(n_exp, 2 * capacity, width_dev)
    all_in, all_grad, far_gate, far_up, far_down, recv = gather_call(
        n_exp, tokens, grad_out, shared_gate, shared_up, shared_down, sends
    )
    n_far = n_exp // NEAR
    width_sh = shared_gate.shape[1]
    all_in, all_grad = all_in.reshape(-1, width_dev), all_grad.reshape(-1, width_dev)
    far_gate = jnp.concatenate([far_gate[k] for k in range(n_far)], axis=1)
    far_up = jnp.concatenate([far_up[k] for k in range(n_far)], axis=1)
    far_down = far_down.reshape(-1, width_dev)
    recv = recv.reshape(n_exp, 2, capacity, width_dev)
    rows_in = recv[:, 0].reshape(n_exp * capacity, width_dev)
    rows_grad = recv[:, 1].reshape(n_exp * capacity, width_dev)
    shared_acts, routed_acts = hidden_call(
        lax.axis_size("dp"),
        partial_products(all_in, all_grad, far_gate, far_up, far_down),
        partial_products(rows_in, rows_grad, w_gate[0], w_up[0], w_down[0]),
    )
    act, grad_gate_pre, grad_up_pre = (
        shared_acts[w].reshape(-1, n_far * width_sh) for w in range(3)
    )
    routed_act, routed_gate, routed_up = (
        routed_acts[w].reshape(n_exp * capacity, -1) for w in range(3)
    )
    me = lax.axis_index("expert")
    far, high, low = me // NEAR, me % NEAR // 2, me % 2

    def columns(value, index):
        return lax.dynamic_slice_in_dim(value, index * width_sh, width_sh, axis=1)

    def own_parts(index):
        return (
            contract_rows(all_in, columns(grad_gate_pre, index)),
            contract_rows(all_in, columns(grad_up_pre, index)),
            contract_rows(columns(act, index), all_grad),
        )

    def send(value, target):
        return lax.ppermute(value, "expert", [(e, target(e)) for e in range(n_exp)])

    got_parts = [
        [
            send(part.astype(jnp.bfloat16), lambda e: (e + k * NEAR) % n_exp)
            for part in own_parts(lax.rem(far + k, n_far))
        ]
        for k in range(1, n_far)
    ]

    def back_of(index):
        def half(value):
            blocks = value.reshape(2, 2, -1, value.shape[1])
            return lax.dynamic_index_in_dim(blocks, index, axis=1, keepdims=False)

        gate_half, up_half = half(grad_gate_pre), half(grad_up_pre)
        rows = gate_half.shape[0] * gate_half.shape[1]
        back = contract_cols(gate_half.reshape(rows, -1), far_gate) + contract_cols(
            up_half.reshape(rows, -1), far_up
        )
        return back.reshape(2, -1, width_dev)

    got_beside = send(back_of(1 - low).astype(jnp.bfloat16), lambda e: e + 1 - e % 2 * 2)
    route_back = contract_cols(routed_gate, w_gate[0]) + contract_cols(routed_up, w_up[0])
    back_rows = lax.all_to_all(
        route_back.astype(jnp.bfloat16).reshape(n_exp, capacity, width_dev),
        "expert",
        split_axis=0,
        concat_axis=0,
        tiled=True,
    )
    pair_back = back_of(low) + got_beside.astype(jnp.float32)
    passed = lax.dynamic_index_in_dim(pair_back, 1 - high, axis=0, keepdims=False)
    kept = lax.dynamic_index_in_dim(pair_back, high, axis=0, keepdims=False)
    got_across = send(passed.astype(jnp.bfloat16), lambda e: e + 2 - e // 2 % 2 * 4)
    routed = jnp.einsum("tec,ecd->td", place_bf, back_rows, preferred_element_type=jnp.float32)
    totals = own_parts(far)
    for parts in got_parts:
        totals = [total + part.astype(jnp.float32) for total, part in zip(totals, parts)]
    return (
        (kept + got_across.astype(jnp.float32) + routed).astype(jnp.bfloat16),
        (contract_rows(rows_in, routed_gate) * grad_scale).astype(jnp.bfloat16)[None],
        (contract_rows(rows_in, routed_up) * grad_scale).astype(jnp.bfloat16)[None],
        (contract_rows(routed_act, rows_grad) * grad_scale).astype(jnp.bfloat16)[None],
        totals[0] * grad_scale,
        totals[1] * grad_scale,
        totals[2] * grad_scale,
    )


def solution(mesh):
    in_specs = (
        P("expert", "dp"),
        P("expert", "dp"),
        P("expert", None),
        P("expert", None),
        P("expert", "dp", None),
        P("expert", "dp", None),
        P("expert", None, "dp"),
        P("dp", "expert"),
        P("dp", "expert"),
        P("expert", "dp"),
    )
    out_specs = (
        P("expert", "dp"),
        P("expert", "dp", None),
        P("expert", "dp", None),
        P("expert", None, "dp"),
        P("dp", "expert"),
        P("dp", "expert"),
        P("expert", "dp"),
    )
    return jax.shard_map(shards, mesh=mesh, in_specs=in_specs, out_specs=out_specs, check_vma=False)
```

```python
import functools

import jax
import jax.numpy as jnp
from jax import lax
from jax.experimental import pallas as pl
from jax.experimental.pallas import tpu as pltpu
from jax.sharding import PartitionSpec as P

CAP = 12
SLOT = 16
NEAR = 4
CHUNKS = 4
MESH = pl.DeviceIdType.MESH
ANY = pl.BlockSpec(memory_space=pl.ANY)
VMEM = pl.BlockSpec(memory_space=pltpu.VMEM)


def silu_parts(pre):
    sigmoid_val = jax.nn.sigmoid(pre)
    return (pre * sigmoid_val, sigmoid_val * (1.0 + pre * (1.0 - sigmoid_val)))


def contract_rows(left, right):
    return lax.dot_general(
        left, right, (((0,), (0,)), ((), ())), preferred_element_type=jnp.float32
    )


def contract_cols(left, right):
    return lax.dot_general(
        left, right, (((1,), (1,)), ((), ())), preferred_element_type=jnp.float32
    )


def hidden_products(part_gate, part_up, part_act):
    silu_val, silu_slope = silu_parts(part_gate)
    activated = (silu_val * part_up).astype(jnp.bfloat16)
    grad_gate_pre = (part_act * part_up * silu_slope).astype(jnp.bfloat16)
    grad_up_pre = (part_act * silu_val).astype(jnp.bfloat16)
    return (activated, grad_gate_pre, grad_up_pre)


def greet(peers):
    barrier = pltpu.get_barrier_semaphore()
    for peer in peers:
        pl.semaphore_signal(barrier, inc=1, device_id=peer, device_id_type=MESH)
    pl.semaphore_wait(barrier, len(peers))


def remote(src, dst, sems, k, peer):
    return pltpu.make_async_remote_copy(
        src_ref=src,
        dst_ref=dst,
        send_sem=sems[0].at[k],
        recv_sem=sems[1].at[k],
        device_id=peer,
        device_id_type=MESH,
    )


def expert_peers(n_exp):
    dp, me = lax.axis_index("dp"), lax.axis_index("expert")
    far, near = me // NEAR, me % NEAR
    high, low = near // 2, near % 2
    n_far = n_exp // NEAR
    base = far * NEAR
    across = (dp, base + (1 - high) * 2 + low)
    beside = (dp, base + high * 2 + 1 - low)
    corner = (dp, base + (1 - high) * 2 + 1 - low)
    distant = [(dp, lax.rem(far + k, n_far) * NEAR + near) for k in range(1, n_far)]
    every = [(dp, lax.rem(me + k, n_exp)) for k in range(1, n_exp)]
    return me, near, far, across, beside, corner, distant, every


def gather_kernel(n_exp, *refs):
    tokens, grads, *weights = refs[:5]
    sends = refs[5]
    all_tokens, all_grads, *all_weights = refs[6:11]
    recv = refs[11]
    near_sems, far_sems, route_sems = refs[12:14], refs[14:16], refs[16:18]
    own_sem = refs[18]
    me, near, far, across, beside, corner, distant, every = expert_peers(n_exp)
    greet(every)
    pairs = ((tokens, all_tokens), (grads, all_grads))
    rows = tokens.shape[0] // CHUNKS
    copies, relays = [], []
    for k, (src, dst) in enumerate(pairs):
        for c in range(CHUNKS):
            at, sem = pl.ds(c * rows, rows), 3 * (k * CHUNKS + c)
            relays.append(remote(src.at[at], dst.at[near, at], near_sems, sem, across))
            copies.append(remote(src.at[at], dst.at[near, at], near_sems, sem + 1, beside))
            relays[-1].start()
            copies[-1].start()
        for p, peer in enumerate(distant):
            for w in ((0, 1), (2,))[k]:
                copies.append(remote(weights[w], all_weights[w].at[far], far_sems, 3 * p + w, peer))
                copies[-1].start()
    for k, peer in enumerate(every):
        copies.append(remote(sends.at[peer[1]], recv.at[me], route_sems, k, peer))
        copies[-1].start()
    own = [
        pltpu.make_async_copy(src, dst, own_sem.at[k])
        for k, (src, dst) in enumerate(
            [(src, dst.at[near]) for src, dst in pairs]
            + [(weights[w], all_weights[w].at[far]) for w in range(3)]
            + [(sends.at[me], recv.at[me])]
        )
    ]
    for copy in own:
        copy.start()
    other = lax.rem(near + 2, NEAR)
    for k, (_, dst) in enumerate(pairs):
        for c in range(CHUNKS):
            block, sem = dst.at[other, pl.ds(c * rows, rows)], 3 * (k * CHUNKS + c)
            relays[k * CHUNKS + c].wait_recv()
            copies.append(remote(block, block, near_sems, sem + 2, beside))
            copies[-1].start()
    for copy in relays:
        copy.wait_send()
    for copy in own:
        copy.wait()
    for copy in copies:
        copy.wait()


def gather_call(n_exp, *args):
    n_far = n_exp // NEAR
    shapes = [(NEAR,) + a.shape for a in args[:2]] + [(n_far,) + a.shape for a in args[2:5]]
    shapes.append(args[5].shape)
    counts = (6 * CHUNKS, 6 * CHUNKS, 3 * (n_far - 1), 3 * (n_far - 1), n_exp - 1, n_exp - 1, 6)
    return pl.pallas_call(
        functools.partial(gather_kernel, n_exp),
        out_shape=[jax.ShapeDtypeStruct(shape, jnp.bfloat16) for shape in shapes],
        in_specs=[ANY] * 6,
        out_specs=[ANY] * 6,
        scratch_shapes=[pltpu.SemaphoreType.DMA((count,)) for count in counts],
        compiler_params=pltpu.CompilerParams(collective_id=1, has_side_effects=True),
    )(*args)


def hidden_kernel(n_dp, *refs):
    parts, outs = refs[:2], refs[2:4]
    met, held, far = refs[4:6], refs[6:8], refs[8:10]
    meet_sems, far_sems, give_sems = refs[10:12], refs[12:14], refs[14:16]
    dp, expert = lax.axis_index("dp"), lax.axis_index("expert")
    chip, core = dp // 2, dp % 2
    chips = n_dp // 2
    twin = (chip * 2 + 1 - core, expert)
    peers = [(lax.rem(chip + k, chips) * 2 + core, expert) for k in range(1, chips)]
    greet([twin] + peers)
    meets = [remote(parts[a].at[:, 1 - core], met[a], meet_sems, a, twin) for a in range(2)]
    for copy in meets:
        copy.start()
    copies = []
    for a in range(2):
        rows = 64 if met[a].shape[1] % 64 == 0 else SLOT
        meets[a].wait()

        @pl.loop(0, met[a].shape[1] // rows)
        def _(step):
            at = pl.ds(pl.multiple_of(step * rows, rows), rows)
            for w in range(3):
                held[a][w, at] = (
                    parts[a][w, core, at].astype(jnp.float32) + met[a][w, at].astype(jnp.float32)
                ).astype(jnp.bfloat16)

        copies.append(
            [
                remote(held[a], far[a].at[k], far_sems, a * (chips - 1) + k, peer)
                for k, peer in enumerate(peers)
            ]
        )
        for copy in copies[-1]:
            copy.start()
    gives = []
    for a in range(2):
        rows = 64 if met[a].shape[1] % 64 == 0 else SLOT
        for copy in copies[a]:
            copy.wait()

        @pl.loop(0, met[a].shape[1] // rows)
        def _(step):
            at = pl.ds(pl.multiple_of(step * rows, rows), rows)
            totals = []
            for w in range(3):
                total = held[a][w, at].astype(jnp.float32)
                for k in range(chips - 1):
                    total = total + far[a][k, w, at].astype(jnp.float32)
                totals.append(total)
            for w, value in enumerate(hidden_products(*totals)):
                outs[a][w, core, at] = value

        gives.append(remote(outs[a].at[:, core], outs[a].at[:, core], give_sems, a, twin))
        gives[-1].start()
    for copy in gives:
        copy.wait()


def hidden_call(n_dp, *args):
    chips = n_dp // 2
    halves = [(3,) + a.shape[2:] for a in args]
    return pl.pallas_call(
        functools.partial(hidden_kernel, n_dp),
        out_shape=[jax.ShapeDtypeStruct(a.shape, jnp.bfloat16) for a in args],
        in_specs=[VMEM] * 2,
        out_specs=[VMEM] * 2,
        scratch_shapes=[pltpu.VMEM(shape, jnp.bfloat16) for shape in halves * 2]
        + [pltpu.VMEM((chips - 1,) + shape, jnp.bfloat16) for shape in halves]
        + [
            pltpu.SemaphoreType.DMA((count,))
            for count in (2, 2, 2 * (chips - 1), 2 * (chips - 1), 2, 2)
        ],
        compiler_params=pltpu.CompilerParams(
            collective_id=3, has_side_effects=True, vmem_limit_bytes=40 * 2**20
        ),
    )(*args)


def partial_products(rows_in, rows_grad, weight_gate, weight_up, weight_down):
    part_gate = jnp.dot(rows_in, weight_gate, preferred_element_type=jnp.float32)
    part_up = jnp.dot(rows_in, weight_up, preferred_element_type=jnp.float32)
    part_act = contract_cols(rows_grad, weight_down)
    parts = jnp.stack([part.astype(jnp.bfloat16) for part in (part_gate, part_up, part_act)])
    rows, width = part_gate.shape
    return parts.reshape(3, 2, rows // 2, width)


def shards(
    tokens,
    grad_out,
    route_ids,
    route_gates,
    w_gate,
    w_up,
    w_down,
    shared_gate,
    shared_up,
    shared_down,
):
    n_exp = lax.axis_size("expert")
    capacity = SLOT
    grad_scale = 1.0 / n_exp
    targets = jnp.arange(n_exp, dtype=jnp.int32)
    matches = route_ids[:, :, None] == targets[None, None, :]
    chosen = jnp.any(matches, axis=1).astype(jnp.int32)
    gate_total = jnp.sum(jnp.where(matches, route_gates[:, :, None], 0.0), axis=1)
    slot_rank = jnp.cumsum(chosen, axis=0) - 1
    slot_ids = jnp.arange(capacity, dtype=jnp.int32)
    placement = (chosen[:, :, None] == 1) & (slot_rank[:, :, None] == slot_ids[None, None, :])
    place_bf = placement.astype(jnp.bfloat16)
    picked_in = jnp.einsum("tec,td->ecd", place_bf, tokens, preferred_element_type=jnp.float32)
    slot_gate = jnp.einsum("tec,te->ec", placement.astype(jnp.float32), gate_total)
    picked_grad = jnp.einsum("tec,td->ecd", place_bf, grad_out, preferred_element_type=jnp.float32)
    picked = jnp.stack([picked_in, slot_gate[:, :, None] * picked_grad], axis=1).astype(jnp.bfloat16)
    width_dev = tokens.shape[1]
    sends = picked.reshape(n_exp, 2 * capacity, width_dev)
    all_in, all_grad, far_gate, far_up, far_down, recv = gather_call(
        n_exp, tokens, grad_out, shared_gate, shared_up, shared_down, sends
    )
    n_far = n_exp // NEAR
    width_sh = shared_gate.shape[1]
    all_in, all_grad = all_in.reshape(-1, width_dev), all_grad.reshape(-1, width_dev)
    far_gate = jnp.concatenate([far_gate[k] for k in range(n_far)], axis=1)
    far_up = jnp.concatenate([far_up[k] for k in range(n_far)], axis=1)
    far_down = far_down.reshape(-1, width_dev)
    recv = recv.reshape(n_exp, 2, capacity, width_dev)
    rows_in = recv[:, 0].reshape(n_exp * capacity, width_dev)
    rows_grad = recv[:, 1].reshape(n_exp * capacity, width_dev)
    shared_acts, routed_acts = hidden_call(
        lax.axis_size("dp"),
        partial_products(all_in, all_grad, far_gate, far_up, far_down),
        partial_products(rows_in, rows_grad, w_gate[0], w_up[0], w_down[0]),
    )
    act, grad_gate_pre, grad_up_pre = (
        shared_acts[w].reshape(-1, n_far * width_sh) for w in range(3)
    )
    routed_act, routed_gate, routed_up = (
        routed_acts[w].reshape(n_exp * capacity, -1) for w in range(3)
    )
    me = lax.axis_index("expert")
    far, high, low = me // NEAR, me % NEAR // 2, me % 2

    def columns(value, index):
        return lax.dynamic_slice_in_dim(value, index * width_sh, width_sh, axis=1)

    def own_parts(index):
        return (
            contract_rows(all_in, columns(grad_gate_pre, index)),
            contract_rows(all_in, columns(grad_up_pre, index)),
            contract_rows(columns(act, index), all_grad),
        )

    def send(value, target):
        return lax.ppermute(value, "expert", [(e, target(e)) for e in range(n_exp)])

    def back_of(index):
        def block(value):
            blocks = value.reshape(NEAR, -1, value.shape[1])
            return lax.dynamic_index_in_dim(blocks, index, axis=0, keepdims=False)

        return contract_cols(block(grad_gate_pre), far_gate) + contract_cols(
            block(grad_up_pre), far_up
        )

    def beside(e):
        return e + 1 - e % 2 * 2

    corner_back = back_of((1 - high) * 2 + 1 - low).astype(jnp.bfloat16)
    corner_back, act, grad_gate_pre, grad_up_pre, routed_gate, routed_up = lax.optimization_barrier(
        (corner_back, act, grad_gate_pre, grad_up_pre, routed_gate, routed_up)
    )
    got_corner = send(corner_back, beside)
    got_parts = [
        [
            send(part.astype(jnp.bfloat16), lambda e: (e + k * NEAR) % n_exp)
            for part in own_parts(lax.rem(far + k, n_far))
        ]
        for k in range(1, n_far)
    ]

    got_beside = send(back_of(high * 2 + 1 - low).astype(jnp.bfloat16), beside)
    route_back = contract_cols(routed_gate, w_gate[0]) + contract_cols(routed_up, w_up[0])
    back_rows = lax.all_to_all(
        route_back.astype(jnp.bfloat16).reshape(n_exp, capacity, width_dev),
        "expert",
        split_axis=0,
        concat_axis=0,
        tiled=True,
    )
    passed = back_of((1 - high) * 2 + low) + got_corner.astype(jnp.float32)
    got_across = send(passed.astype(jnp.bfloat16), lambda e: e + 2 - e // 2 % 2 * 4)
    kept = back_of(me % NEAR) + got_beside.astype(jnp.float32)
    routed = jnp.einsum("tec,ecd->td", place_bf, back_rows, preferred_element_type=jnp.float32)
    totals = own_parts(far)
    for parts in got_parts:
        totals = [total + part.astype(jnp.float32) for total, part in zip(totals, parts)]
    return (
        (kept + got_across.astype(jnp.float32) + routed).astype(jnp.bfloat16),
        (contract_rows(rows_in, routed_gate) * grad_scale).astype(jnp.bfloat16)[None],
        (contract_rows(rows_in, routed_up) * grad_scale).astype(jnp.bfloat16)[None],
        (contract_rows(routed_act, rows_grad) * grad_scale).astype(jnp.bfloat16)[None],
        totals[0] * grad_scale,
        totals[1] * grad_scale,
        totals[2] * grad_scale,
    )


def solution(mesh):
    in_specs = (
        P("expert", "dp"),
        P("expert", "dp"),
        P("expert", None),
        P("expert", None),
        P("expert", "dp", None),
        P("expert", "dp", None),
        P("expert", None, "dp"),
        P("dp", "expert"),
        P("dp", "expert"),
        P("expert", "dp"),
    )
    out_specs = (
        P("expert", "dp"),
        P("expert", "dp", None),
        P("expert", "dp", None),
        P("expert", None, "dp"),
        P("dp", "expert"),
        P("dp", "expert"),
        P("expert", "dp"),
    )
    return jax.shard_map(shards, mesh=mesh, in_specs=in_specs, out_specs=out_specs, check_vma=False)
```
